256 devices in a mesh: lat: 64 (over z, x_hi, y), tok: 4 (over x_lo, core).
Axes of the slice: x: 4 (x_hi: 2, x_lo: 2; x = x_hi * 2 + x_lo), y: 4, z: 8, core: 2. Of those that a mesh axis runs over, the one named last changes fastest.
Arguments:
- activations: bfloat16 [2048, 4608], P('tok', 'lat'), may hold values from -6 to 6
- enc_weight: bfloat16 [4608, 32768], P(None, 'lat'), may hold values from -6 to 6
- enc_bias: float32 [32768], P('lat'), may hold values from -1.5 to 0.5
- dec_weight: bfloat16 [32768, 4608], P('lat'), may hold values from -16 to 16
- dec_bias: float32 [4608], replicated, may hold values from -3 to 3
- learning_rate: float32 [1], replicated, may hold values from 0.2 to 0.4
Outputs:
- recon_error: bfloat16 [2048, 4608], P('tok', 'lat')
- new_enc: bfloat16 [4608, 32768], P('tok', 'lat')
- new_dec: bfloat16 [32768, 4608], P(('lat', 'tok'))
The draws below stay inside these ranges and needn't reach their ends.
All inputs are finite; a program needn't handle non-finite values.
Results may differ from the reference program's by a relative error of at most 0.015.
Values may be sent and summed in bfloat16 or wider, within the bound.
No kernel may reach another device: no remote copies, remote signals or barrier semaphores. Data moves between devices by JAX's collectives and lax.ppermute only.
A program may use at most 128 MiB of HBM per device.

```python
import math
import jax
import jax.numpy as jnp
from jax import lax

D = 4608
TOK_DEV = 512
LATENTS = 32768
TOKENS = 2048
N_TOK = 4


def raised(values, rng, source, target, parts, factor):
    owner, partner = [(jnp.arange(values.shape[axis_at]) // (values.shape[axis_at] // parts)).reshape([-1 if axis == axis_at else 1 for axis in range(values.ndim)]) for axis_at in (source, target)]
    chosen = jax.random.permutation(rng, parts)[partner]
    strong = (owner == chosen) | (owner == (partner + parts // 2) % parts)
    return jnp.where(strong, factor * values, values)


def level_of(own_key, extent, pieces, low, largest):
    loudness, own = 1.0, jax.random.fold_in(own_key, 6)
    for dim, shards_of in pieces:
        steps = jnp.exp(jax.random.uniform(jax.random.fold_in(own, dim), (shards_of,), jnp.float32, low / len(pieces), largest / len(pieces)))
        loudness = loudness * jnp.repeat(steps, extent[dim] // shards_of).reshape([-1 if axis == dim else 1 for axis in range(len(extent))])
    return loudness


def noise(stream_key, extent, deviation, most, cuts=(), held_as=jnp.bfloat16):
    result = jax.random.normal(stream_key, extent, jnp.float32) * deviation
    if len(cuts) > 0:
        result = level_of(stream_key, extent, cuts, -0.22, 0.18) * result
    return jnp.clip(result, min=-most, max=most).astype(held_as)


def bell_draw_with(rng, shape, width, limit, shards, heavy, dtype=jnp.bfloat16):
    array = width * jax.random.normal(rng, shape, jnp.float32)
    if shards:
        array = array * level_of(rng, shape, shards, -0.22, 0.18)
    return jnp.clip(raised(array, jax.random.fold_in(rng, 3), *heavy), -limit, limit).astype(dtype)


def setup_inputs(seed: int = 0) -> dict:
    arg_keys = jax.random.split(jax.random.key(seed), 7)
    activations = noise(arg_keys[0], (TOKENS, D), 1.0, 6.0, ((0, 4), (1, 64)))
    enc_weight = noise(arg_keys[1], (D, LATENTS), 1.0, 6.0, ((1, 64),))
    enc_bias = jnp.clip(-1.5 + 2.0 * jax.random.uniform(arg_keys[2], (LATENTS,), jnp.float32) ** level_of(arg_keys[2], (LATENTS,), ((0, 64),), -0.2, 0.2), -1.5, 0.5)
    dec_weight = bell_draw_with(arg_keys[3], (LATENTS, D), 1.0, 16.0, ((0, 64),), (0, 1, 64, 4.0))
    dec_bias = noise(arg_keys[4], (D,), 0.5, 3.0, (), jnp.float32)
    learning_rate = jnp.clip(jax.random.uniform(arg_keys[5], (1,), jnp.float32, 0.2, 0.4), 0.2, 0.4)
    return {"activations": activations, "enc_weight": enc_weight, "enc_bias": enc_bias, "dec_weight": dec_weight, "dec_bias": dec_bias, "learning_rate": learning_rate}


sparsity_coef = 0.2

def reference(activations, enc_weight, enc_bias, dec_weight, dec_bias, learning_rate):
    enc_scale = 1.0 / math.sqrt(D)
    dec_scale = 2.0 / math.sqrt(LATENTS)
    preact = jnp.dot(activations, enc_weight, preferred_element_type=jnp.float32) * enc_scale + enc_bias
    latent_codes = jnp.maximum(preact, 0.0).astype(jnp.bfloat16)
    recon = jnp.dot(latent_codes, dec_weight, preferred_element_type=jnp.float32) * dec_scale + dec_bias
    recon_error = (recon - activations.astype(jnp.float32)).astype(jnp.bfloat16)
    grad_codes = (jnp.dot(recon_error, dec_weight.T, preferred_element_type=jnp.float32) * dec_scale + sparsity_coef) / TOKENS
    grad_pre = jnp.where(preact > 0.0, grad_codes, 0.0).astype(jnp.bfloat16)
    enc_grad = jnp.zeros((D, LATENTS), jnp.float32)
    dec_grad = jnp.zeros((LATENTS, D), jnp.float32)
    for tok_block in range(N_TOK):
        first_row = tok_block * TOK_DEV
        act_block = activations[first_row:first_row + TOK_DEV]
        pre_block = grad_pre[first_row:first_row + TOK_DEV]
        code_block = latent_codes[first_row:first_row + TOK_DEV]
        error_block = recon_error[first_row:first_row + TOK_DEV]
        enc_part = jnp.dot(act_block.T, pre_block, preferred_element_type=jnp.float32) * enc_scale
        dec_part = jnp.dot(code_block.T, error_block, preferred_element_type=jnp.float32) * (dec_scale / TOKENS)
        enc_grad = enc_grad + lax.optimization_barrier(enc_part.astype(jnp.bfloat16)).astype(jnp.float32)
        dec_grad = dec_grad + lax.optimization_barrier(dec_part.astype(jnp.bfloat16)).astype(jnp.float32)
    step_rate = learning_rate[0] * math.sqrt(TOKENS * LATENTS)
    new_enc = (enc_weight.astype(jnp.float32) - step_rate * enc_grad).astype(jnp.bfloat16)
    new_dec = (dec_weight.astype(jnp.float32) - step_rate * dec_grad).astype(jnp.bfloat16)
    return (recon_error, new_enc, new_dec)
```

```python
import math

import jax
import jax.numpy as jnp
from jax import lax
from jax.sharding import PartitionSpec as P

sparsity_coef = 0.2
NZ, NX, NY = 8, 2, 4
bf16, f32 = jnp.bfloat16, jnp.float32


def lat_pairs(move):
    pairs = []
    for z in range(NZ):
        for x in range(NX):
            for y in range(NY):
                a, b, c = move(z, x, y)
                pairs.append((z * 8 + x * 4 + y, (a % NZ) * 8 + (b % NX) * 4 + c % NY))
    return pairs


def shift_z(v, k):
    return lax.ppermute(v, "lat", lat_pairs(lambda z, x, y: (z + k, x, y)))


def shift_y(v, k):
    return lax.ppermute(v, "lat", lat_pairs(lambda z, x, y: (z, x, y + k)))


def swap_xh(v):
    return lax.ppermute(v, "lat", lat_pairs(lambda z, x, y: (z, x + 1, y)))


def swap_tok(v, bits):
    return lax.ppermute(v, "tok", [(t, t ^ bits) for t in range(4)])


def swap_near(v):
    pairs = []
    for s, d in lat_pairs(lambda z, x, y: (z, x + 1, y)):
        for t in range(4):
            pairs.append((s * 4 + t, d * 4 + (t ^ 2)))
    return lax.ppermute(v, ("lat", "tok"), pairs)


def in_order(blocks, start):
    n = len(blocks)
    twice = jnp.stack(blocks + blocks[:-1])
    return lax.dynamic_slice_in_dim(twice, (n - start) % n, n, 0)


def pick(v, index, axis=0):
    return lax.dynamic_index_in_dim(v, index, axis, keepdims=False)


def gather_ring(block, n, me, shift):
    buf = jnp.zeros((n,) + block.shape, block.dtype)
    put = lambda b, v, k: lax.dynamic_update_index_in_dim(b, v, (me + k) % n, 0)
    buf = put(buf, block, 0)
    left = right = block
    for k in range(1, n // 2):
        left = shift(left, 1)
        right = shift(right, -1)
        buf = put(buf, left, n - k)
        buf = put(buf, right, k)
    half = block.shape[0] // 2
    a = shift(left[:half], 1)
    b = shift(right[half:], -1)
    far = jnp.concatenate([a, b], 0)
    return put(buf, far, n // 2)


def scatter_ring(parts, n, me, shift):
    half = parts.shape[1] // 2
    at = lambda k: pick(parts, (me + k) % n)
    far = at(n // 2)
    up = shift(far[:half], 1)
    down = shift(far[half:], -1)
    for k in range(n // 2 - 1, 0, -1):
        own_up, own_down = at(k), at(n - k)
        if k == n // 2 - 1:
            own_up = jnp.concatenate([own_up[:half] + up, own_up[half:]], 0)
            own_down = jnp.concatenate([own_down[:half], own_down[half:] + down], 0)
        else:
            own_up, own_down = own_up + up, own_down + down
        up, down = shift(own_up, 1), shift(own_down, -1)
    return at(0) + up + down


def gather_direct(block, n, me, shift):
    return in_order([block] + [shift(block, -k) for k in range(1, n)], me)


def scatter_direct(parts, n, me, shift):
    total = pick(parts, me)
    for k in range(1, n):
        total = total + shift(pick(parts, (me + k) % n), k)
    return total


def local(activations, enc_weight, enc_bias, dec_weight, dec_bias, learning_rate):
    lat_total = lax.axis_size("lat")
    tok_total = lax.axis_size("tok")
    T = activations.shape[0]
    D, L = enc_weight.shape
    latent_total = L * lat_total
    token_total = T * tok_total
    C = D // lat_total
    CB = (C * 4 // 9) // 8 * 8 if C >= 16 else C // 2
    CA = C - CB
    enc_scale = 1.0 / math.sqrt(D)
    dec_scale = 2.0 / math.sqrt(latent_total)
    lat = lax.axis_index("lat")
    tok = lax.axis_index("tok")
    z, xh, y = lat // 8, (lat // 4) % 2, lat % 4
    core, xl = tok % 2, tok // 2

    def dot(a, b, ca, cb):
        return lax.dot_general(a, b, (((ca,), (cb,)), ((), ())), preferred_element_type=f32)

    def gather(own_a, own_b):
        a = gather_direct(own_a, NY, y, shift_y)
        a = in_order([a, swap_xh(a)], xh)
        a = gather_ring(a.reshape(-1, T), NZ, z, shift_z)
        b = gather_direct(own_b, NZ, z, shift_z)
        other = swap_xh(b)
        b = jnp.where(xh == 0, jnp.stack([b, other], 1), jnp.stack([other, b], 1))
        b = gather_ring(b.reshape(-1, T), NY, y, shift_y)
        return a.reshape(-1, T), b.reshape(-1, T)

    def rows_a(w):
        w = w.reshape(NZ, NX, NY, C, -1)[:, :, :, :CA]
        return w

    def rows_b(w):
        w = w.reshape(NZ, NX, NY, C, -1)[:, :, :, CA:]
        return w.transpose(2, 0, 1, 3, 4)

    act_t = activations.T
    act_a, act_b = gather(act_t[:CA], act_t[CA:])

    dec_t = dec_weight.T.reshape(NZ, NX, NY, C, L)
    dec_mine = pick(dec_t, xh, 1)
    dec_give = pick(dec_t, 1 - xh, 1)
    give = lax.dynamic_slice_in_dim(dec_give, core * (NZ // 2), NZ // 2, 0)
    got = swap_near(give)
    got_core = swap_tok(got, 1)
    dec_other = in_order([got, got_core], core).reshape(NZ, NY, C, L)

    preact = (
        dot(rows_a(enc_weight).reshape(-1, L), act_a, 0, 0)
        + dot(rows_b(enc_weight).reshape(-1, L), act_b, 0, 0)
    ) * enc_scale + enc_bias[:, None]
    codes = jnp.maximum(preact, 0.0).astype(bf16)
    codes_other = swap_xh(codes)

    def rows_for(a, b, t):
        ra = lax.dynamic_slice_in_dim(a.reshape(NZ, NX * NY * CA, T), t * 2, 2, 0)
        rb = lax.dynamic_slice_in_dim(b.reshape(NY, NZ, NX * CB, T), t * 2, 2, 1)
        return jnp.concatenate([ra.reshape(-1, T), rb.reshape(-1, T)], 0)

    def half_a(w):
        return w[:, :, :CA].reshape(-1, L)

    def half_b(w):
        return w[:, :, CA:].transpose(1, 0, 2, 3).reshape(-1, L)

    part_a = dot(half_a(dec_mine), codes, 1, 0) + dot(half_a(dec_other), codes_other, 1, 0)
    part_b = dot(half_b(dec_mine), codes, 1, 0) + dot(half_b(dec_other), codes_other, 1, 0)
    sum_a = scatter_ring(part_a.reshape(NZ, NY * CA, T), NZ, z, shift_z).reshape(NY, CA, T)
    sum_a = scatter_direct(sum_a, NY, y, shift_y)
    sum_b = scatter_ring(part_b.reshape(NY, NZ * CB, T), NY, y, shift_y).reshape(NZ, CB, T)
    sum_b = scatter_direct(sum_b, NZ, z, shift_z)
    bias = lax.dynamic_slice_in_dim(dec_bias, lat * C, C, 0)[:, None]

    def error_of(total, lo, hi):
        return (total * dec_scale + bias[lo:hi] - act_t[lo:hi].astype(f32)).astype(bf16)

    own_a, own_b = error_of(sum_a, 0, CA), error_of(sum_b, CA, C)
    error_own = jnp.concatenate([own_a, own_b], 0).T
    err_a, err_b = gather(own_a, own_b)

    held_a, held_b, _ = lax.optimization_barrier((act_a, act_b, codes_other))
    act_rows = [rows_for(act_a, act_b, tok)] + [
        swap_tok(rows_for(held_a, held_b, tok ^ k), k) for k in (1, 2, 3)
    ]

    back = dot(rows_a(dec_t).reshape(-1, L), err_a, 0, 0) + dot(
        rows_b(dec_t).reshape(-1, L), err_b, 0, 0
    )
    grad_codes = (back * dec_scale + sparsity_coef) / token_total
    grad_pre = jnp.where(preact > 0.0, grad_codes, 0.0).astype(bf16)
    far = swap_tok(grad_pre, 2)
    grads = [grad_pre, swap_tok(grad_pre, 1), far, swap_tok(far, 1)]
    enc_grad = sum(dot(r, g, 1, 1) for r, g in zip(act_rows, grads)) * enc_scale

    Q = L // tok_total
    quarters = codes.reshape(tok_total, Q, T)
    codes_rel = jnp.concatenate([pick(quarters, tok ^ k) for k in (0, 2, 1, 3)], 0)

    def dec_sum(err):
        product = (dot(err, codes_rel, 1, 1) * (dec_scale / token_total)).astype(bf16)
        near = product[:, : 2 * Q].astype(f32) + swap_tok(product[:, 2 * Q :], 1).astype(f32)
        return near[:, :Q] + swap_tok(near[:, Q:].astype(bf16), 2).astype(f32)

    dec_a = dec_sum(err_a).reshape(NZ, NX, NY, CA, Q)
    dec_b = dec_sum(err_b).reshape(NY, NZ, NX, CB, Q).transpose(1, 2, 0, 3, 4)
    dec_grad = jnp.concatenate([dec_a, dec_b], 3).reshape(D, Q).T

    rows_enc = D // tok_total
    cut = 2 * NX * NY * CA
    enc_a = enc_grad[:cut].reshape(2, NX, NY, CA, L)
    enc_b = enc_grad[cut:].reshape(NY, 2, NX, CB, L).transpose(1, 2, 0, 3, 4)
    enc_grad = jnp.concatenate([enc_a, enc_b], 3).reshape(rows_enc, L)

    step_rate = learning_rate[0] * math.sqrt(token_total * latent_total)
    own_enc = lax.dynamic_slice_in_dim(enc_weight, tok * rows_enc, rows_enc, 0)
    own_dec = lax.dynamic_slice_in_dim(dec_weight, tok * Q, Q, 0)
    new_enc = (own_enc.astype(f32) - step_rate * enc_grad).astype(bf16)
    new_dec = (own_dec.astype(f32) - step_rate * dec_grad).astype(bf16)
    return (error_own, new_enc, new_dec)


def solution(mesh):
    in_specs = (P("tok", "lat"), P(None, "lat"), P("lat"), P("lat", None), P(), P())
    out_specs = (P("tok", "lat"), P("tok", "lat"), P(("lat", "tok"), None))
    return jax.shard_map(local, mesh=mesh, in_specs=in_specs, out_specs=out_specs, check_vma=False)
```

```python
import math

import jax
import jax.numpy as jnp
from jax import lax
from jax.experimental import pallas as pl
from jax.experimental.pallas import tpu as pltpu
from jax.sharding import Mesh
from jax.sharding import PartitionSpec as P

sparsity_coef = 0.2
NZ, NX, NY, NL, NC = 8, 2, 4, 2, 2
bf16, f32 = jnp.bfloat16, jnp.float32
INTERPRET = False


def shift(v, axis, n, k):
    return lax.ppermute(v, axis, [(i, (i + k) % n) for i in range(n)])


def shift_z(v, k):
    return shift(v, "z", NZ, k)


def shift_y(v, k):
    return shift(v, "y", NY, k)


def flip_z(v):
    return lax.ppermute(v, "z", [(i, i ^ 1) for i in range(NZ)])


def swap_xh(v):
    return shift(v, "xh", NX, 1)


def swap_core(v):
    return shift(v, "core", NC, 1)


def swap_xl(v):
    return shift(v, "xl", NL, 1)


def swap_both(v):
    return lax.ppermute(v, ("xl", "core"), [(t, t ^ 3) for t in range(4)])


def swap_near(v):
    return lax.ppermute(v, ("xh", "xl"), [(i, 3 - i) for i in range(4)])


def pick(v, index, axis=0):
    return lax.dynamic_index_in_dim(v, index, axis, keepdims=False)


VMEM = pl.BlockSpec(memory_space=pltpu.VMEM)
SMEM = pl.BlockSpec(memory_space=pltpu.SMEM)
WAIT = pl.BlockSpec(memory_space=pl.ANY)
PARAMS = pltpu.CompilerParams(vmem_limit_bytes=40 * 2**20)


def place(blocks, start, inner=False):
    n = len(blocks)

    def body(start_ref, *refs):
        for k in range(n):
            at = (start_ref[0] + k) % n
            if inner:
                for i in range(blocks[0].shape[0]):
                    refs[n][i, at] = refs[k][i]
            else:
                refs[n][at] = refs[k][...]

    shape = blocks[0].shape
    shape = (shape[0], n) + shape[1:] if inner else (n,) + shape
    return pl.pallas_call(
        body,
        out_shape=jax.ShapeDtypeStruct(shape, blocks[0].dtype),
        in_specs=[SMEM] + [VMEM] * n,
        out_specs=VMEM,
        compiler_params=PARAMS,
        interpret=INTERPRET,
    )(start.reshape(1), *blocks)


def gather_ring(block, z):
    buf = jnp.zeros((NZ,) + block.shape, block.dtype)
    put = lambda b, v, k: lax.dynamic_update_index_in_dim(b, v, (z + k) % NZ, 0)
    buf = put(buf, block, 0)
    low = high = block
    for k in range(1, NZ // 2):
        low, high = shift_z(low, 1), shift_z(high, -1)
        buf = put(put(buf, low, NZ - k), high, k)
    half = block.shape[0] // 2
    far = jnp.concatenate([shift_z(low[:half], 1), shift_z(high[half:], -1)], 0)
    return put(buf, far, NZ // 2)


def ring_step(parts, up, down, z, k, *tokens):
    n, rows, T = parts.shape
    half = up.shape[0]

    def body(z_ref, up_part, down_part, up_ref, down_ref, *refs):
        up_out, down_out = refs[-2:]
        if half == rows:
            up_out[...] = up_part[0] + up_ref[...]
            down_out[...] = down_part[0] + down_ref[...]
        else:
            up_out[:half] = up_part[0, :half] + up_ref[...]
            up_out[half:] = up_part[0, half:]
            down_out[:half] = down_part[0, :half]
            down_out[half:] = down_part[0, half:] + down_ref[...]

    full = lambda r: pl.BlockSpec((r, T), lambda i, z_ref: (0, 0))
    return pl.pallas_call(
        body,
        grid_spec=pltpu.PrefetchScalarGridSpec(
            num_scalar_prefetch=1,
            grid=(1,),
            in_specs=[
                pl.BlockSpec((1, rows, T), lambda i, z_ref: ((z_ref[0] + k) % n, 0, 0)),
                pl.BlockSpec((1, rows, T), lambda i, z_ref: ((z_ref[0] + n - k) % n, 0, 0)),
                full(half),
                full(half),
            ]
            + [WAIT] * len(tokens),
            out_specs=[full(rows), full(rows)],
        ),
        out_shape=[jax.ShapeDtypeStruct((rows, T), f32)] * 2,
        compiler_params=PARAMS,
        cost_estimate=cost(2 * rows * T, 24 * rows * T),
        interpret=INTERPRET,
    )(z.reshape(1), parts, parts, up, down, *tokens)


def ring_first(parts, z):
    half = parts.shape[1] // 2
    far = pick(parts, (z + NZ // 2) % NZ)
    return shift_z(far[:half], 1), shift_z(far[half:], -1)


def scatter_ring(parts, up, down, z, token):
    for k in range(NZ // 2 - 1, 0, -1):
        up, down = ring_step(parts, up, down, z, k, *([token] if k == 1 else []))
        up, down = shift_z(up, 1), shift_z(down, -1)
    return pick(parts, z) + up + down


def by_tok(codes, tok):
    n, (L, T) = len(codes), codes[0].shape
    Q = L // 4

    def body(tok_ref, *refs):
        for i, q in enumerate((0, 2, 1, 3)):
            from_row = pl.multiple_of((tok_ref[0] ^ q) * Q, Q)
            for k in range(n):
                refs[n][pl.ds((i * n + k) * Q, Q), :] = refs[k][pl.ds(from_row, Q), :]

    return pl.pallas_call(
        body,
        out_shape=jax.ShapeDtypeStruct((n * L, T), codes[0].dtype),
        in_specs=[SMEM] + [VMEM] * n,
        out_specs=VMEM,
        compiler_params=PARAMS,
        interpret=INTERPRET,
    )(tok.reshape(1), *codes)


def cost(flops, size):
    return pl.CostEstimate(flops=1, bytes_accessed=1, transcendentals=0)


def dot(a, b, ca, cb):
    return lax.dot_general(a, b, (((ca,), (cb,)), ((), ())), preferred_element_type=f32)


def slabs_of(dec, y, core, token):
    L, D = dec.shape
    C, R = D // (NZ * NX * NY), D // NY

    def body(place_ref, dec_ref, token_ref, *refs):
        outs, scratch = refs[:NY], refs[NY]
        scratch[...] = dec_ref[...].T.astype(f32)
        for k in range(NY):
            at = (place_ref[0] + k) % NY
            for i in range(2):
                rows = [
                    scratch[pl.ds(pl.multiple_of(((i * NX + x) * NY + at) * C, 8), C), :]
                    for x in range(NX)
                ]
                block = jnp.concatenate(rows, 0).astype(bf16)
                if k > 0:
                    block = jnp.where(place_ref[1] == 0, block[:, : L // 2], block[:, L // 2 :])
                outs[k][i * NX * C : (i + 1) * NX * C, :] = block

    widths = [L] + [L // 2] * (NY - 1)
    return pl.pallas_call(
        body,
        grid=(4,),
        out_shape=[jax.ShapeDtypeStruct((R, w), bf16) for w in widths],
        in_specs=[SMEM, pl.BlockSpec((L, D // 4), lambda i: (0, i)), WAIT],
        out_specs=[pl.BlockSpec((R // 4, w), lambda i: (i, 0)) for w in widths],
        scratch_shapes=[pltpu.VMEM((D // 4, L), f32)],
        compiler_params=PARAMS,
        cost_estimate=cost(0, 4 * L * D),
        interpret=INTERPRET,
    )(jnp.stack([y, core]), dec, token)


def join(blocks, token):
    rows, w = blocks[0].shape
    n = len(blocks)

    def body(*refs):
        for k in range(n):
            refs[n + 1][:, k * w : (k + 1) * w] = refs[k][...]

    return pl.pallas_call(
        body,
        grid=(2,),
        out_shape=jax.ShapeDtypeStruct((rows, n * w), blocks[0].dtype),
        in_specs=[pl.BlockSpec((rows // 2, w), lambda i: (i, 0))] * n + [WAIT],
        out_specs=pl.BlockSpec((rows // 2, n * w), lambda i: (i, 0)),
        compiler_params=PARAMS,
        cost_estimate=cost(0, 4 * n * rows * w),
        interpret=INTERPRET,
    )(*blocks, token)


def assemble(own, near, other, core):
    R, L = own.shape
    n, h = len(near), L // 2

    def body(core_ref, own_ref, *refs):
        nears, rest, out = refs[:n], refs[n], refs[n + 1]
        out[:, :L] = own_ref[...]
        for k in range(n):
            mine, his = nears[k][...], rest[:, k * h : (k + 1) * h]
            at = (k + 1) * L
            out[:, at : at + h] = jnp.where(core_ref[0] == 0, mine, his)
            out[:, at + h : at + L] = jnp.where(core_ref[0] == 0, his, mine)

    rows = lambda w: pl.BlockSpec((R // 4, w), lambda i: (i, 0))
    return pl.pallas_call(
        body,
        grid=(4,),
        out_shape=jax.ShapeDtypeStruct((R, (n + 1) * L), own.dtype),
        in_specs=[SMEM, rows(L)] + [rows(h)] * n + [rows(n * h)],
        out_specs=rows((n + 1) * L),
        compiler_params=PARAMS,
        cost_estimate=cost(0, 4 * R * (n + 1) * L),
        interpret=INTERPRET,
    )(core.reshape(1), own, *near, other)


def part_of(decs, codes):
    n, (L, T), R = len(codes), codes[0].shape, decs.shape[0]

    def body(w_ref, *refs):
        refs[n][...] = sum(
            dot(w_ref[:, k * L : (k + 1) * L], refs[k][...], 1, 0) for k in range(n)
        )

    return pl.pallas_call(
        body,
        grid=(4,),
        out_shape=jax.ShapeDtypeStruct((R, T), f32),
        in_specs=[pl.BlockSpec((R // 4, n * L), lambda i: (i, 0))]
        + [pl.BlockSpec((L, T), lambda i: (0, 0))] * n,
        out_specs=pl.BlockSpec((R // 4, T), lambda i: (i, 0)),
        compiler_params=PARAMS,
        cost_estimate=cost(2 * R * n * L * T, 2 * R * n * L + 4 * R * T),
        interpret=INTERPRET,
    )(decs, *codes)


def error_of(total, received, bias, act, xh, scale, *tokens):
    rows, T = total.shape
    C = rows // NX

    def body(xh_ref, total_ref, received_ref, bias_ref, act_ref, *refs):
        value = (total_ref[...] + received_ref[...]) * scale + bias_ref[...]
        value = value - act_ref[...].astype(f32)
        refs[-2][...] = value.astype(bf16)
        refs[-1][...] = jnp.where(xh_ref[0] == 0, value[:C], value[C:]).astype(bf16)

    return pl.pallas_call(
        body,
        out_shape=[jax.ShapeDtypeStruct((r, T), bf16) for r in (rows, C)],
        in_specs=[SMEM] + [VMEM] * 4 + [WAIT] * len(tokens),
        out_specs=[VMEM] * 2,
        compiler_params=PARAMS,
        cost_estimate=cost(4 * rows * T, 16 * rows * T),
        interpret=INTERPRET,
    )(xh.reshape(1), total, received, bias, act, *tokens)


def backs_of(decs, err, n, token):
    (R, W), T = decs.shape, err.shape[1]
    L = W // n

    def body(*refs):
        e = refs[n][...]
        for k in range(n):
            refs[n + 2 + k][...] = dot(refs[k][...], e, 0, 0).astype(bf16)

    return pl.pallas_call(
        body,
        grid=(2,),
        out_shape=[jax.ShapeDtypeStruct((L, T), bf16)] * n,
        in_specs=[pl.BlockSpec((R, L // 2), lambda i, k=k: (0, 2 * k + i)) for k in range(n)]
        + [pl.BlockSpec((R, T), lambda i: (0, 0)), WAIT],
        out_specs=[pl.BlockSpec((L // 2, T), lambda i: (i, 0))] * n,
        compiler_params=PARAMS,
        cost_estimate=cost(2 * R * W * T, 2 * W * (R + T)),
        interpret=INTERPRET,
    )(*([decs] * n), err, token)


def dec_product(err, codes, scale, token):
    (R, T), W = err.shape, codes.shape[0]

    def body(err_ref, codes_ref, token_ref, keep_ref, send_ref):
        e = err_ref[...]
        keep_ref[...] = (dot(e, codes_ref[: W // 2, :], 1, 1) * scale).astype(bf16)
        send_ref[...] = (dot(e, codes_ref[W // 2 :, :], 1, 1) * scale).astype(bf16)

    rows = lambda w: pl.BlockSpec((R // 4, w), lambda i: (i, 0))
    return pl.pallas_call(
        body,
        grid=(4,),
        out_shape=[jax.ShapeDtypeStruct((R, W // 2), bf16)] * 2,
        in_specs=[rows(T), pl.BlockSpec((W, T), lambda i: (0, 0)), WAIT],
        out_specs=[rows(W // 2)] * 2,
        compiler_params=PARAMS,
        cost_estimate=cost(2 * R * W * T, 2 * R * W + 2 * W * T),
        interpret=INTERPRET,
    )(err, codes, token)


def near_sum(keep, received, token):
    rows, W = keep.shape

    def body(keep_ref, received_ref, token_ref, mine_ref, send_ref):
        total = keep_ref[...].astype(f32) + received_ref[...].astype(f32)
        mine_ref[...] = total[:, : W // 2]
        send_ref[...] = total[:, W // 2 :].astype(bf16)

    block = lambda w: pl.BlockSpec((rows // 4, w), lambda i: (i, 0))
    return pl.pallas_call(
        body,
        grid=(4,),
        out_shape=[jax.ShapeDtypeStruct((rows, W // 2), d) for d in (f32, bf16)],
        in_specs=[block(W), block(W), WAIT],
        out_specs=[block(W // 2), block(W // 2)],
        compiler_params=PARAMS,
        cost_estimate=cost(rows * W, 7 * rows * W),
        interpret=INTERPRET,
    )(keep, received, token)


def far_sum(mine, received, *tokens):
    rows, W = mine.shape
    Q = W // NY

    def body(mine_ref, received_ref, *refs):
        outs = refs[len(tokens) :]
        total = (mine_ref[...] + received_ref[...].astype(f32)).astype(bf16)
        for k in range(NY):
            outs[k][...] = total[:, k * Q : (k + 1) * Q]

    return pl.pallas_call(
        body,
        out_shape=[jax.ShapeDtypeStruct((rows, Q), bf16)] * NY,
        in_specs=[VMEM, VMEM] + [WAIT] * len(tokens),
        out_specs=[VMEM] * NY,
        compiler_params=PARAMS,
        cost_estimate=cost(rows * W, 8 * rows * W),
        interpret=INTERPRET,
    )(mine, received, *tokens)


def grad_of(parts, preact, scale, coef, count, *tokens):
    L, T = preact.shape
    n = len(parts)

    def body(*refs):
        total = refs[0][...].astype(f32)
        for k in range(1, n):
            total = total + refs[k][...].astype(f32)
        grad = (total * scale + coef) / count
        refs[-1][...] = jnp.where(refs[n][...] > 0.0, grad, 0.0).astype(bf16)

    return pl.pallas_call(
        body,
        out_shape=jax.ShapeDtypeStruct((L, T), bf16),
        in_specs=[VMEM] * (n + 1) + [WAIT] * len(tokens),
        out_specs=VMEM,
        compiler_params=PARAMS,
        cost_estimate=cost(8 * L * T, 14 * L * T),
        interpret=INTERPRET,
    )(*parts, preact, *tokens)


def rows_of(act, tok, token):
    D, T = act.shape
    block = D // 16

    def body(at_ref, act_ref, token_ref, out_ref):
        out_ref[...] = act_ref[...]

    return pl.pallas_call(
        body,
        grid_spec=pltpu.PrefetchScalarGridSpec(
            num_scalar_prefetch=1,
            grid=(4,),
            in_specs=[pl.BlockSpec((block, T), lambda i, at_ref: (at_ref[0] * 4 + i, 0)), WAIT],
            out_specs=pl.BlockSpec((block, T), lambda i, at_ref: (i, 0)),
        ),
        out_shape=jax.ShapeDtypeStruct((4 * block, T), act.dtype),
        compiler_params=PARAMS,
        cost_estimate=cost(0, D * T),
        interpret=INTERPRET,
    )(tok.reshape(1), act, token)


def rows_above(act, tok, more):
    D, T = act.shape
    block = D // 16

    def body(at_ref, act_ref, more_ref, out_ref):
        above = pl.program_id(0) < 4
        out_ref[...] = jnp.where(above, act_ref[...], more_ref[...])

    def top(i, at_ref):
        return (at_ref[0] * 4 + jnp.minimum(i, 3), 0)

    return pl.pallas_call(
        body,
        grid_spec=pltpu.PrefetchScalarGridSpec(
            num_scalar_prefetch=1,
            grid=(8,),
            in_specs=[
                pl.BlockSpec((block, T), top),
                pl.BlockSpec((block, T), lambda i, at_ref: (jnp.maximum(i - 4, 0), 0)),
            ],
            out_specs=pl.BlockSpec((block, T), lambda i, at_ref: (i, 0)),
        ),
        out_shape=jax.ShapeDtypeStruct((8 * block, T), act.dtype),
        compiler_params=PARAMS,
        cost_estimate=cost(0, 2 * D * T),
        interpret=INTERPRET,
    )(tok.reshape(1), act, more)


def hold(x, *tokens):
    def body(x_ref, *refs):
        refs[-1][...] = x_ref[...]

    return pl.pallas_call(
        body,
        out_shape=jax.ShapeDtypeStruct(x.shape, x.dtype),
        in_specs=[VMEM] + [WAIT] * len(tokens),
        out_specs=VMEM,
        compiler_params=PARAMS,
        cost_estimate=cost(0, 4 * x.size),
        interpret=INTERPRET,
    )(x, *tokens)


def enc_first(act, tok, act_core, grads):
    (D, T), L = act.shape, grads[0].shape[0]
    rows = D // 16

    def body(tok_ref, act_ref, core_ref, own_grad, core_grad, out_ref):
        out_ref[...] = dot(act_ref[...], own_grad[...], 1, 1) + dot(
            core_ref[...], core_grad[...], 1, 1
        )

    full = pl.BlockSpec((L, T), lambda i, tok_ref: (0, 0))
    return pl.pallas_call(
        body,
        grid_spec=pltpu.PrefetchScalarGridSpec(
            num_scalar_prefetch=1,
            grid=(4,),
            in_specs=[
                pl.BlockSpec((rows, T), lambda i, tok_ref: (tok_ref[0] * 4 + i, 0)),
                pl.BlockSpec((rows, T), lambda i, tok_ref: (i, 0)),
                full,
                full,
            ],
            out_specs=pl.BlockSpec((rows, L), lambda i, tok_ref: (i, 0)),
        ),
        out_shape=jax.ShapeDtypeStruct((4 * rows, L), f32),
        compiler_params=PARAMS,
        cost_estimate=cost(16 * rows * T * L, 16 * rows * L),
        interpret=INTERPRET,
    )(tok.reshape(1), act, act_core, *grads)


def enc_update(first, act_xl, act_core, grads, enc, tok, rate, scale):
    (rows, L), T = first.shape, act_xl.shape[1]

    def body(tok_ref, rate_ref, first_ref, enc_ref, xl_ref, both_ref, xl_grad, both_grad, out_ref):
        total = first_ref[...] + dot(xl_ref[...], xl_grad[...], 1, 1)
        total = total + dot(both_ref[...], both_grad[...], 1, 1)
        step = rate_ref[0] * scale
        out_ref[...] = (enc_ref[...].astype(f32) - step * total).astype(bf16)

    block = lambda w: pl.BlockSpec((rows // 4, w), lambda i, tok_ref: (i, 0))
    full = pl.BlockSpec((L, T), lambda i, tok_ref: (0, 0))
    return pl.pallas_call(
        body,
        grid_spec=pltpu.PrefetchScalarGridSpec(
            num_scalar_prefetch=1,
            grid=(4,),
            in_specs=[
                SMEM,
                block(L),
                pl.BlockSpec((rows // 4, L), lambda i, tok_ref: (tok_ref[0] * 4 + i, 0)),
                block(T),
                pl.BlockSpec((rows // 4, T), lambda i, tok_ref: (4 + i, 0)),
                full,
                full,
            ],
            out_specs=block(L),
        ),
        out_shape=jax.ShapeDtypeStruct((rows, L), bf16),
        compiler_params=PARAMS,
        cost_estimate=cost(4 * rows * T * L, 16 * rows * L),
        interpret=INTERPRET,
    )(tok.reshape(1), rate, first, enc, act_xl, act_core, *grads)


def dec_update(grads, dec, tok, y, rate, token):
    (rows, Q), D = grads[0].shape, dec.shape[1]
    C = D // (NZ * NX * NY)
    n = len(grads)

    def body(at_ref, rate_ref, dec_ref, *refs):
        out, scratch = refs[n + 1 :]
        for k in range(n):
            value = refs[k][...].astype(f32)
            to = (at_ref[1] + k) % NY
            for g in range(rows // C):
                row = (g * NY + to) * C
                scratch[pl.ds(pl.multiple_of(row, 8), C), :] = value[g * C : (g + 1) * C]
        step = rate_ref[0]
        for i in range(4):
            at = slice(i * (D // 4), (i + 1) * (D // 4))
            new = dec_ref[:, at].astype(f32) - step * scratch[at, :].T
            out[:, at] = new.astype(bf16)

    full = pl.BlockSpec((rows, Q), lambda i, at_ref: (0, 0))
    return pl.pallas_call(
        body,
        grid_spec=pltpu.PrefetchScalarGridSpec(
            num_scalar_prefetch=1,
            grid=(1,),
            in_specs=[SMEM, pl.BlockSpec((Q, D), lambda i, at_ref: (at_ref[0], 0))]
            + [full] * n
            + [WAIT],
            out_specs=pl.BlockSpec((Q, D), lambda i, at_ref: (0, 0)),
            scratch_shapes=[pltpu.VMEM((D, Q), f32)],
        ),
        out_shape=jax.ShapeDtypeStruct((Q, D), bf16),
        compiler_params=PARAMS,
        cost_estimate=cost(2 * Q * D, 6 * Q * D),
        interpret=INTERPRET,
    )(jnp.stack([tok, y]), rate, dec, *grads, token)


def local(activations, enc_weight, enc_bias, dec_weight, dec_bias, learning_rate):
    T = activations.shape[0]
    D, L = enc_weight.shape
    latent_total = L * NZ * NX * NY
    token_total = T * NL * NC
    C = D // (NZ * NX * NY)
    enc_scale = 1.0 / math.sqrt(D)
    dec_scale = 2.0 / math.sqrt(latent_total)
    z, xh, y = lax.axis_index("z"), lax.axis_index("xh"), lax.axis_index("y")
    xl, core = lax.axis_index("xl"), lax.axis_index("core")
    tok = xl * NC + core

    act_t = activations.T
    pair = place([act_t, swap_xh(act_t)], xh)
    quad = place([pair] + [shift_y(pair, -k) for k in range(1, NY)], y, inner=True)
    act = gather_ring(quad.reshape(NX * NY * C, T), z).reshape(D, T)

    R = NZ * NX * C
    slabs = slabs_of(dec_weight, y, core, quad)
    dec_own = slabs[0]
    dec_near = [shift_y(slabs[NY - k], -k) for k in range(1, NY)]

    preact = dot(enc_weight, act, 0, 0) * enc_scale + enc_bias[:, None]
    codes = jnp.maximum(preact, 0.0).astype(bf16)
    codes_all = [codes] + [shift_y(codes, -k) for k in range(1, NY)]
    dec_other = swap_core(join(dec_near, codes))
    decs = assemble(dec_own, dec_near, dec_other, core)

    part = part_of(decs, codes_all)
    act_xl = swap_xl(rows_of(act, tok ^ 2, decs))
    act_far = swap_xl(rows_of(act, tok ^ 3, part))
    part = part.reshape(NZ, NX * C, T)
    up, down = ring_first(part, z)
    total = scatter_ring(part, up, down, z, act_xl)
    codes_rel = by_tok(codes_all, tok)
    bias = dec_bias.reshape(NZ, NX, NY, C)
    bias = pick(pick(bias, z), y, 1).reshape(NX * C, 1)
    errors, error_own = error_of(
        total, swap_xh(total), bias, pair.reshape(NX * C, T), xh, dec_scale, codes_rel, act_far
    )
    error_own = error_own.T
    act_core = swap_core(rows_above(act, tok ^ 1, act_far))
    err = gather_ring(errors, z).reshape(R, T)

    keep, send = dec_product(err, codes_rel, dec_scale / token_total, act_core)

    backs = backs_of(decs, err, NY, keep)
    received = [shift_y(backs[k], k) for k in range(1, NY)]

    mine, send = near_sum(keep, swap_core(send), backs[1])
    got = swap_xl(send)
    sums = far_sum(mine, got)
    grad_pre = grad_of(
        [backs[0], *received], preact, dec_scale, sparsity_coef, token_total, sums[0]
    )
    sums = [sums[0]] + [shift_y(sums[k], k) for k in range(1, NY)]
    sums = sums[:1] + sums[:0:-1]

    far = swap_xl(grad_pre)
    first = enc_first(act, tok, act_core, [grad_pre, swap_core(grad_pre)])
    far = hold(far, first, *sums[1:])
    rate = learning_rate * math.sqrt(token_total * latent_total)
    new_enc = enc_update(
        first, act_xl, act_core, [far, swap_core(far)], enc_weight, tok, rate, enc_scale
    )
    new_dec = dec_update(sums, dec_weight, tok, y, rate, new_enc)
    return (error_own, new_enc, new_dec)


def solution(mesh):
    fine = Mesh(mesh.devices.reshape(NZ, NX, NY, NL, NC), ("z", "xh", "y", "xl", "core"))
    lat, tok = ("z", "xh", "y"), ("xl", "core")
    in_specs = (P(tok, lat), P(None, lat), P(lat), P(lat, None), P(), P())
    out_specs = (P(tok, lat), P(tok, lat), P(lat + tok, None))
    return jax.shard_map(local, mesh=fine, in_specs=in_specs, out_specs=out_specs, check_vma=False)
```

```python
import math

import jax
import jax.numpy as jnp
from jax import lax
from jax.experimental import pallas as pl
from jax.experimental.pallas import tpu as pltpu
from jax.sharding import Mesh
from jax.sharding import PartitionSpec as P

sparsity_coef = 0.2
NZ, NX, NY, NL, NC = 8, 2, 4, 2, 2
bf16, f32 = jnp.bfloat16, jnp.float32
INTERPRET = False


def shift(v, axis, n, k):
    return lax.ppermute(v, axis, [(i, (i + k) % n) for i in range(n)])


def shift_z(v, k):
    return shift(v, "z", NZ, k)


def shift_y(v, k):
    return shift(v, "y", NY, k)


def flip_z(v):
    return lax.ppermute(v, "z", [(i, i ^ 1) for i in range(NZ)])


def swap_xh(v):
    return shift(v, "xh", NX, 1)


def swap_core(v):
    return shift(v, "core", NC, 1)


def swap_xl(v):
    return shift(v, "xl", NL, 1)


def swap_both(v):
    return lax.ppermute(v, ("xl", "core"), [(t, t ^ 3) for t in range(4)])


def swap_near(v):
    return lax.ppermute(v, ("xh", "xl"), [(i, 3 - i) for i in range(4)])


def pick(v, index, axis=0):
    return lax.dynamic_index_in_dim(v, index, axis, keepdims=False)


VMEM = pl.BlockSpec(memory_space=pltpu.VMEM)
SMEM = pl.BlockSpec(memory_space=pltpu.SMEM)
WAIT = pl.BlockSpec(memory_space=pl.ANY)
PARAMS = pltpu.CompilerParams(vmem_limit_bytes=20 * 2**20)


def place(blocks, start, inner=False):
    n = len(blocks)

    def body(start_ref, *refs):
        for k in range(n):
            at = (start_ref[0] + k) % n
            if inner:
                for i in range(blocks[0].shape[0]):
                    refs[n][i, at] = refs[k][i]
            else:
                refs[n][at] = refs[k][...]

    shape = blocks[0].shape
    shape = (shape[0], n) + shape[1:] if inner else (n,) + shape
    return pl.pallas_call(
        body,
        out_shape=jax.ShapeDtypeStruct(shape, blocks[0].dtype),
        in_specs=[SMEM] + [VMEM] * n,
        out_specs=VMEM,
        compiler_params=PARAMS,
        interpret=INTERPRET,
    )(start.reshape(1), *blocks)


def gather_ring(block, z):
    buf = jnp.zeros((NZ,) + block.shape, block.dtype)
    put = lambda b, v, k: lax.dynamic_update_index_in_dim(b, v, (z + k) % NZ, 0)
    buf = put(buf, block, 0)
    low = high = block
    for k in range(1, NZ // 2):
        low, high = shift_z(low, 1), shift_z(high, -1)
        buf = put(put(buf, low, NZ - k), high, k)
    half = block.shape[0] // 2
    far = jnp.concatenate([shift_z(low[:half], 1), shift_z(high[half:], -1)], 0)
    return put(buf, far, NZ // 2)


def ring_step(parts, up, down, z, k, *tokens):
    n, rows, T = parts.shape
    half = up.shape[0]

    def body(z_ref, up_part, down_part, up_ref, down_ref, *refs):
        up_out, down_out = refs[-2:]
        if half == rows:
            up_out[...] = up_part[0] + up_ref[...]
            down_out[...] = down_part[0] + down_ref[...]
        else:
            up_out[:half] = up_part[0, :half] + up_ref[...]
            up_out[half:] = up_part[0, half:]
            down_out[:half] = down_part[0, :half]
            down_out[half:] = down_part[0, half:] + down_ref[...]

    full = lambda r: pl.BlockSpec((r, T), lambda i, z_ref: (0, 0))
    return pl.pallas_call(
        body,
        grid_spec=pltpu.PrefetchScalarGridSpec(
            num_scalar_prefetch=1,
            grid=(1,),
            in_specs=[
                pl.BlockSpec((1, rows, T), lambda i, z_ref: ((z_ref[0] + k) % n, 0, 0)),
                pl.BlockSpec((1, rows, T), lambda i, z_ref: ((z_ref[0] + n - k) % n, 0, 0)),
                full(half),
                full(half),
            ]
            + [WAIT] * len(tokens),
            out_specs=[full(rows), full(rows)],
        ),
        out_shape=[jax.ShapeDtypeStruct((rows, T), f32)] * 2,
        compiler_params=PARAMS,
        cost_estimate=cost(2 * rows * T, 24 * rows * T),
        interpret=INTERPRET,
    )(z.reshape(1), parts, parts, up, down, *tokens)


def ring_first(parts, z):
    half = parts.shape[1] // 2
    far = pick(parts, (z + NZ // 2) % NZ)
    return shift_z(far[:half], 1), shift_z(far[half:], -1)


def scatter_ring(parts, up, down, z, token):
    for k in range(NZ // 2 - 1, 0, -1):
        up, down = ring_step(parts, up, down, z, k, *([token] if k == 1 else []))
        up, down = shift_z(up, 1), shift_z(down, -1)
    return pick(parts, z) + up + down


def by_tok(codes, tok):
    n, (L, T) = len(codes), codes[0].shape
    Q = L // 4

    def body(tok_ref, *refs):
        for i, q in enumerate((0, 2, 1, 3)):
            from_row = pl.multiple_of((tok_ref[0] ^ q) * Q, Q)
            for k in range(n):
                refs[n][pl.ds((i * n + k) * Q, Q), :] = refs[k][pl.ds(from_row, Q), :]

    return pl.pallas_call(
        body,
        out_shape=jax.ShapeDtypeStruct((n * L, T), codes[0].dtype),
        in_specs=[SMEM] + [VMEM] * n,
        out_specs=VMEM,
        compiler_params=PARAMS,
        interpret=INTERPRET,
    )(tok.reshape(1), *codes)


def cost(flops, size):
    return pl.CostEstimate(flops=1, bytes_accessed=1, transcendentals=0)


def dot(a, b, ca, cb):
    return lax.dot_general(a, b, (((ca,), (cb,)), ((), ())), preferred_element_type=f32)


def slabs_of(dec, y, core, token):
    L, D = dec.shape
    C, R = D // (NZ * NX * NY), D // NY

    def body(place_ref, dec_ref, token_ref, *refs):
        outs, scratch = refs[:NY], refs[NY]
        scratch[...] = dec_ref[...].T.astype(f32)
        for k in range(NY):
            at = (place_ref[0] + k) % NY
            for i in range(2):
                rows = [
                    scratch[pl.ds(pl.multiple_of(((i * NX + x) * NY + at) * C, 8), C), :]
                    for x in range(NX)
                ]
                block = jnp.concatenate(rows, 0).astype(bf16)
                if k > 0:
                    block = jnp.where(place_ref[1] == 0, block[:, : L // 2], block[:, L // 2 :])
                outs[k][i * NX * C : (i + 1) * NX * C, :] = block

    widths = [L] + [L // 2] * (NY - 1)
    return pl.pallas_call(
        body,
        grid=(4,),
        out_shape=[jax.ShapeDtypeStruct((R, w), bf16) for w in widths],
        in_specs=[SMEM, pl.BlockSpec((L, D // 4), lambda i: (0, i)), WAIT],
        out_specs=[pl.BlockSpec((R // 4, w), lambda i: (i, 0)) for w in widths],
        scratch_shapes=[pltpu.VMEM((D // 4, L), f32)],
        compiler_params=PARAMS,
        cost_estimate=cost(0, 4 * L * D),
        interpret=INTERPRET,
    )(jnp.stack([y, core]), dec, token)


def join(blocks, token):
    rows, w = blocks[0].shape
    n = len(blocks)

    def body(*refs):
        for k in range(n):
            refs[n + 1][:, k * w : (k + 1) * w] = refs[k][...]

    return pl.pallas_call(
        body,
        grid=(2,),
        out_shape=jax.ShapeDtypeStruct((rows, n * w), blocks[0].dtype),
        in_specs=[pl.BlockSpec((rows // 2, w), lambda i: (i, 0))] * n + [WAIT],
        out_specs=pl.BlockSpec((rows // 2, n * w), lambda i: (i, 0)),
        compiler_params=PARAMS,
        cost_estimate=cost(0, 4 * n * rows * w),
        interpret=INTERPRET,
    )(*blocks, token)


def assemble(own, near, other, core):
    R, L = own.shape
    n, h = len(near), L // 2

    def body(core_ref, own_ref, *refs):
        nears, rest, out = refs[:n], refs[n], refs[n + 1]
        out[:, :L] = own_ref[...]
        for k in range(n):
            mine, his = nears[k][...], rest[:, k * h : (k + 1) * h]
            at = (k + 1) * L
            out[:, at : at + h] = jnp.where(core_ref[0] == 0, mine, his)
            out[:, at + h : at + L] = jnp.where(core_ref[0] == 0, his, mine)

    rows = lambda w: pl.BlockSpec((R // 4, w), lambda i: (i, 0))
    return pl.pallas_call(
        body,
        grid=(4,),
        out_shape=jax.ShapeDtypeStruct((R, (n + 1) * L), own.dtype),
        in_specs=[SMEM, rows(L)] + [rows(h)] * n + [rows(n * h)],
        out_specs=rows((n + 1) * L),
        compiler_params=PARAMS,
        cost_estimate=cost(0, 4 * R * (n + 1) * L),
        interpret=INTERPRET,
    )(core.reshape(1), own, *near, other)


def part_of(decs, codes):
    n, (L, T), R = len(codes), codes[0].shape, decs.shape[0]

    def body(w_ref, *refs):
        refs[n][...] = sum(
            dot(w_ref[:, k * L : (k + 1) * L], refs[k][...], 1, 0) for k in range(n)
        )

    return pl.pallas_call(
        body,
        grid=(4,),
        out_shape=jax.ShapeDtypeStruct((R, T), f32),
        in_specs=[pl.BlockSpec((R // 4, n * L), lambda i: (i, 0))]
        + [pl.BlockSpec((L, T), lambda i: (0, 0))] * n,
        out_specs=pl.BlockSpec((R // 4, T), lambda i: (i, 0)),
        compiler_params=PARAMS,
        cost_estimate=cost(2 * R * n * L * T, 2 * R * n * L + 4 * R * T),
        interpret=INTERPRET,
    )(decs, *codes)


def error_of(total, received, bias, act, xh, scale, *tokens):
    rows, T = total.shape
    C = rows // NX

    def body(xh_ref, total_ref, received_ref, bias_ref, act_ref, *refs):
        value = (total_ref[...] + received_ref[...]) * scale + bias_ref[...]
        value = value - act_ref[...].astype(f32)
        refs[-2][...] = value.astype(bf16)
        refs[-1][...] = jnp.where(xh_ref[0] == 0, value[:C], value[C:]).astype(bf16)

    return pl.pallas_call(
        body,
        out_shape=[jax.ShapeDtypeStruct((r, T), bf16) for r in (rows, C)],
        in_specs=[SMEM] + [VMEM] * 4 + [WAIT] * len(tokens),
        out_specs=[VMEM] * 2,
        compiler_params=PARAMS,
        cost_estimate=cost(4 * rows * T, 16 * rows * T),
        interpret=INTERPRET,
    )(xh.reshape(1), total, received, bias, act, *tokens)


def backs_of(decs, err, n, token):
    (R, W), T = decs.shape, err.shape[1]
    L = W // n

    def body(*refs):
        e = refs[n][...]
        for k in range(n):
            refs[n + 2 + k][...] = dot(refs[k][...], e, 0, 0).astype(bf16)

    return pl.pallas_call(
        body,
        grid=(2,),
        out_shape=[jax.ShapeDtypeStruct((L, T), bf16)] * n,
        in_specs=[pl.BlockSpec((R, L // 2), lambda i, k=k: (0, 2 * k + i)) for k in range(n)]
        + [pl.BlockSpec((R, T), lambda i: (0, 0)), WAIT],
        out_specs=[pl.BlockSpec((L // 2, T), lambda i: (i, 0))] * n,
        compiler_params=PARAMS,
        cost_estimate=cost(2 * R * W * T, 2 * W * (R + T)),
        interpret=INTERPRET,
    )(*([decs] * n), err, token)


def dec_product(err, codes, scale):
    (R, T), W = err.shape, codes.shape[0]

    def body(err_ref, codes_ref, keep_ref, send_ref):
        e = err_ref[...]
        keep_ref[...] = (dot(e, codes_ref[: W // 2, :], 1, 1) * scale).astype(bf16)
        send_ref[...] = (dot(e, codes_ref[W // 2 :, :], 1, 1) * scale).astype(bf16)

    rows = lambda w: pl.BlockSpec((R // 4, w), lambda i: (i, 0))
    return pl.pallas_call(
        body,
        grid=(4,),
        out_shape=[jax.ShapeDtypeStruct((R, W // 2), bf16)] * 2,
        in_specs=[rows(T), pl.BlockSpec((W, T), lambda i: (0, 0))],
        out_specs=[rows(W // 2)] * 2,
        compiler_params=PARAMS,
        cost_estimate=cost(2 * R * W * T, 2 * R * W + 2 * W * T),
        interpret=INTERPRET,
    )(err, codes)


def near_sum(keep, received, token):
    rows, W = keep.shape

    def body(keep_ref, received_ref, token_ref, mine_ref, send_ref):
        total = keep_ref[...].astype(f32) + received_ref[...].astype(f32)
        mine_ref[...] = total[:, : W // 2]
        send_ref[...] = total[:, W // 2 :].astype(bf16)

    block = lambda w: pl.BlockSpec((rows // 4, w), lambda i: (i, 0))
    return pl.pallas_call(
        body,
        grid=(4,),
        out_shape=[jax.ShapeDtypeStruct((rows, W // 2), d) for d in (f32, bf16)],
        in_specs=[block(W), block(W), WAIT],
        out_specs=[block(W // 2), block(W // 2)],
        compiler_params=PARAMS,
        cost_estimate=cost(rows * W, 7 * rows * W),
        interpret=INTERPRET,
    )(keep, received, token)


def far_sum(mine, received, *tokens):
    rows, W = mine.shape
    Q = W // NY

    def body(mine_ref, received_ref, *refs):
        outs = refs[len(tokens) :]
        total = (mine_ref[...] + received_ref[...].astype(f32)).astype(bf16)
        for k in range(NY):
            outs[k][...] = total[:, k * Q : (k + 1) * Q]

    return pl.pallas_call(
        body,
        out_shape=[jax.ShapeDtypeStruct((rows, Q), bf16)] * NY,
        in_specs=[VMEM, VMEM] + [WAIT] * len(tokens),
        out_specs=[VMEM] * NY,
        compiler_params=PARAMS,
        cost_estimate=cost(rows * W, 8 * rows * W),
        interpret=INTERPRET,
    )(mine, received, *tokens)


def grad_of(parts, preact, scale, coef, count, *tokens):
    L, T = preact.shape
    n = len(parts)

    def body(*refs):
        total = refs[0][...].astype(f32)
        for k in range(1, n):
            total = total + refs[k][...].astype(f32)
        grad = (total * scale + coef) / count
        refs[-1][...] = jnp.where(refs[n][...] > 0.0, grad, 0.0).astype(bf16)

    return pl.pallas_call(
        body,
        out_shape=jax.ShapeDtypeStruct((L, T), bf16),
        in_specs=[VMEM] * (n + 1) + [WAIT] * len(tokens),
        out_specs=VMEM,
        compiler_params=PARAMS,
        cost_estimate=cost(8 * L * T, 14 * L * T),
        interpret=INTERPRET,
    )(*parts, preact, *tokens)


def rows_of(act, tok, token):
    D, T = act.shape
    rows = D // 4

    def body(at_ref, act_ref, token_ref, out_ref, sem):
        first = pl.multiple_of(at_ref[0] * rows, rows)
        copy = pltpu.make_async_copy(act_ref.at[pl.ds(first, rows)], out_ref, sem)
        copy.start()
        copy.wait()

    return pl.pallas_call(
        body,
        out_shape=jax.ShapeDtypeStruct((rows, T), act.dtype),
        in_specs=[SMEM, WAIT, WAIT],
        out_specs=WAIT,
        scratch_shapes=[pltpu.SemaphoreType.DMA],
        compiler_params=PARAMS,
        cost_estimate=cost(0, D * T),
        interpret=INTERPRET,
    )(tok.reshape(1), act, token)


def rows_above(act, tok, more, token):
    D, T = act.shape
    rows = D // 4

    def body(at_ref, act_ref, more_ref, token_ref, out_ref, sems):
        first = pl.multiple_of(at_ref[0] * rows, rows)
        copies = [
            pltpu.make_async_copy(
                act_ref.at[pl.ds(first, rows)], out_ref.at[pl.ds(0, rows)], sems.at[0]
            ),
            pltpu.make_async_copy(more_ref, out_ref.at[pl.ds(rows, rows)], sems.at[1]),
        ]
        for copy in copies:
            copy.start()
        for copy in copies:
            copy.wait()

    return pl.pallas_call(
        body,
        out_shape=jax.ShapeDtypeStruct((2 * rows, T), act.dtype),
        in_specs=[SMEM, WAIT, WAIT, WAIT],
        out_specs=WAIT,
        scratch_shapes=[pltpu.SemaphoreType.DMA((2,))],
        compiler_params=PARAMS,
        cost_estimate=cost(0, 2 * D * T),
        interpret=INTERPRET,
    )(tok.reshape(1), act, more, token)


def hold(x, *tokens):
    def body(x_ref, *refs):
        refs[-1][...] = x_ref[...]

    return pl.pallas_call(
        body,
        out_shape=jax.ShapeDtypeStruct(x.shape, x.dtype),
        in_specs=[VMEM] + [WAIT] * len(tokens),
        out_specs=VMEM,
        compiler_params=PARAMS,
        cost_estimate=cost(0, 4 * x.size),
        interpret=INTERPRET,
    )(x, *tokens)


def enc_first(act, tok, act_core, grads):
    (D, T), L = act.shape, grads[0].shape[0]
    rows = D // 16

    def body(tok_ref, act_ref, core_ref, own_grad, core_grad, out_ref):
        out_ref[...] = dot(act_ref[...], own_grad[...], 1, 1) + dot(
            core_ref[...], core_grad[...], 1, 1
        )

    full = pl.BlockSpec((L, T), lambda i, tok_ref: (0, 0))
    return pl.pallas_call(
        body,
        grid_spec=pltpu.PrefetchScalarGridSpec(
            num_scalar_prefetch=1,
            grid=(4,),
            in_specs=[
                pl.BlockSpec((rows, T), lambda i, tok_ref: (tok_ref[0] * 4 + i, 0)),
                pl.BlockSpec((rows, T), lambda i, tok_ref: (i, 0)),
                full,
                full,
            ],
            out_specs=pl.BlockSpec((rows, L), lambda i, tok_ref: (i, 0)),
        ),
        out_shape=jax.ShapeDtypeStruct((4 * rows, L), f32),
        compiler_params=PARAMS,
        cost_estimate=cost(16 * rows * T * L, 16 * rows * L),
        interpret=INTERPRET,
    )(tok.reshape(1), act, act_core, *grads)


def enc_update(first, act_xl, act_core, grads, enc, rate, scale):
    (rows, L), T = first.shape, act_xl.shape[1]

    def body(rate_ref, first_ref, enc_ref, xl_ref, both_ref, xl_grad, both_grad, out_ref):
        total = first_ref[...] + dot(xl_ref[...], xl_grad[...], 1, 1)
        total = total + dot(both_ref[...], both_grad[...], 1, 1)
        step = rate_ref[0] * scale
        out_ref[...] = (enc_ref[...].astype(f32) - step * total).astype(bf16)

    block = lambda w: pl.BlockSpec((rows // 4, w), lambda i: (i, 0))
    full = pl.BlockSpec((L, T), lambda i: (0, 0))
    return pl.pallas_call(
        body,
        grid=(4,),
        in_specs=[
            SMEM,
            block(L),
            block(L),
            block(T),
            pl.BlockSpec((rows // 4, T), lambda i: (4 + i, 0)),
            full,
            full,
        ],
        out_specs=block(L),
        out_shape=jax.ShapeDtypeStruct((rows, L), bf16),
        compiler_params=PARAMS,
        cost_estimate=cost(4 * rows * T * L, 16 * rows * L),
        interpret=INTERPRET,
    )(rate, first, enc, act_xl, act_core, *grads)


def dec_update(grads, dec, tok, y, rate):
    (rows, Q), D = grads[0].shape, dec.shape[1]
    C = D // (NZ * NX * NY)
    n = len(grads)

    def body(at_ref, rate_ref, dec_ref, *refs):
        out, scratch = refs[n:]
        for k in range(n):
            value = refs[k][...].astype(f32)
            to = (at_ref[1] + k) % NY
            for g in range(rows // C):
                row = (g * NY + to) * C
                scratch[pl.ds(pl.multiple_of(row, 8), C), :] = value[g * C : (g + 1) * C]
        step = rate_ref[0]
        for i in range(4):
            at = slice(i * (D // 4), (i + 1) * (D // 4))
            new = dec_ref[:, at].astype(f32) - step * scratch[at, :].T
            out[:, at] = new.astype(bf16)

    full = pl.BlockSpec((rows, Q), lambda i, at_ref: (0, 0))
    return pl.pallas_call(
        body,
        grid_spec=pltpu.PrefetchScalarGridSpec(
            num_scalar_prefetch=1,
            grid=(1,),
            in_specs=[SMEM, pl.BlockSpec((Q, D), lambda i, at_ref: (at_ref[0], 0))]
            + [full] * n,
            out_specs=pl.BlockSpec((Q, D), lambda i, at_ref: (0, 0)),
            scratch_shapes=[pltpu.VMEM((D, Q), f32)],
        ),
        out_shape=jax.ShapeDtypeStruct((Q, D), bf16),
        compiler_params=PARAMS,
        cost_estimate=cost(2 * Q * D, 6 * Q * D),
        interpret=INTERPRET,
    )(jnp.stack([tok, y]), rate, dec, *grads)


def local(activations, enc_weight, enc_bias, dec_weight, dec_bias, learning_rate):
    T = activations.shape[0]
    D, L = enc_weight.shape
    latent_total = L * NZ * NX * NY
    token_total = T * NL * NC
    C = D // (NZ * NX * NY)
    enc_scale = 1.0 / math.sqrt(D)
    dec_scale = 2.0 / math.sqrt(latent_total)
    z, xh, y = lax.axis_index("z"), lax.axis_index("xh"), lax.axis_index("y")
    xl, core = lax.axis_index("xl"), lax.axis_index("core")
    tok = xl * NC + core

    act_t = activations.T
    pair = place([act_t, swap_xh(act_t)], xh)
    quad = place([pair] + [shift_y(pair, -k) for k in range(1, NY)], y, inner=True)
    act = gather_ring(quad.reshape(NX * NY * C, T), z).reshape(D, T)

    R = NZ * NX * C
    slabs = slabs_of(dec_weight, y, core, quad)
    dec_own = slabs[0]
    dec_near = [shift_y(slabs[NY - k], -k) for k in range(1, NY)]

    preact = dot(enc_weight, act, 0, 0) * enc_scale + enc_bias[:, None]
    codes = jnp.maximum(preact, 0.0).astype(bf16)
    codes_all = [codes] + [shift_y(codes, -k) for k in range(1, NY)]
    dec_other = swap_core(join(dec_near, codes))
    decs = assemble(dec_own, dec_near, dec_other, core)

    part = part_of(decs, codes_all)
    act_xl = swap_xl(rows_of(act, tok ^ 2, decs))
    part = part.reshape(NZ, NX * C, T)
    up, down = ring_first(part, z)
    act_far = swap_xl(rows_of(act, tok ^ 3, up))
    total = scatter_ring(part, up, down, z, act_xl)
    codes_rel = by_tok(codes_all, tok)
    rows = rows_above(act, tok ^ 1, act_far, total)
    act_core = swap_core(rows)
    bias = dec_bias.reshape(NZ, NX, NY, C)
    bias = pick(pick(bias, z), y, 1).reshape(NX * C, 1)
    errors, error_own = error_of(
        total, swap_xh(total), bias, pair.reshape(NX * C, T), xh, dec_scale, codes_rel, rows
    )
    error_own = error_own.T
    err = gather_ring(errors, z).reshape(R, T)

    keep, send = dec_product(err, codes_rel, dec_scale / token_total)

    backs = backs_of(decs, err, NY, keep)
    received = [shift_y(backs[k], k) for k in range(1, NY)]

    mine, send = near_sum(keep, swap_core(send), backs[1])
    got = swap_xl(send)
    enc_own = rows_of(enc_weight, tok, mine)
    sums = far_sum(mine, got)
    grad_pre = grad_of(
        [backs[0], *received], preact, dec_scale, sparsity_coef, token_total, sums[0]
    )
    sums = [sums[0]] + [shift_y(sums[k], k) for k in range(1, NY)]
    sums = sums[:1] + sums[:0:-1]

    far = swap_xl(grad_pre)
    first = enc_first(act, tok, act_core, [grad_pre, swap_core(grad_pre)])
    far = hold(far, first, enc_own, *sums[1:])
    rate = learning_rate * math.sqrt(token_total * latent_total)
    new_dec = dec_update(sums, dec_weight, tok, y, rate)
    new_enc = enc_update(
        first, act_xl, act_core, [far, swap_core(far)], enc_own, rate, enc_scale
    )
    return (error_own, new_enc, new_dec)


def solution(mesh):
    fine = Mesh(mesh.devices.reshape(NZ, NX, NY, NL, NC), ("z", "xh", "y", "xl", "core"))
    lat, tok = ("z", "xh", "y"), ("xl", "core")
    in_specs = (P(tok, lat), P(None, lat), P(lat), P(lat, None), P(), P())
    out_specs = (P(tok, lat), P(tok, lat), P(lat + tok, None))
    return jax.shard_map(local, mesh=fine, in_specs=in_specs, out_specs=out_specs, check_vma=False)
```

```python
import math

import jax
import jax.numpy as jnp
from jax import lax
from jax.experimental import pallas as pl
from jax.experimental.pallas import tpu as pltpu
from jax.sharding import Mesh
from jax.sharding import PartitionSpec as P

sparsity_coef = 0.2
NZ, NX, NY, NL, NC = 8, 2, 4, 2, 2
bf16, f32 = jnp.bfloat16, jnp.float32
INTERPRET = False


def shift(v, axis, n, k):
    return lax.ppermute(v, axis, [(i, (i + k) % n) for i in range(n)])


def shift_z(v, k):
    return shift(v, "z", NZ, k)


def shift_y(v, k):
    return shift(v, "y", NY, k)


def flip_z(v):
    return lax.ppermute(v, "z", [(i, i ^ 1) for i in range(NZ)])


def swap_xh(v):
    return shift(v, "xh", NX, 1)


def swap_core(v):
    return shift(v, "core", NC, 1)


def swap_xl(v):
    return shift(v, "xl", NL, 1)


def swap_both(v):
    return lax.ppermute(v, ("xl", "core"), [(t, t ^ 3) for t in range(4)])


def swap_near(v):
    return lax.ppermute(v, ("xh", "xl"), [(i, 3 - i) for i in range(4)])


def pick(v, index, axis=0):
    return lax.dynamic_index_in_dim(v, index, axis, keepdims=False)


VMEM = pl.BlockSpec(memory_space=pltpu.VMEM)
SMEM = pl.BlockSpec(memory_space=pltpu.SMEM)
WAIT = pl.BlockSpec(memory_space=pl.ANY)
PARAMS = pltpu.CompilerParams(vmem_limit_bytes=20 * 2**20)


def place(blocks, start, inner=False):
    n = len(blocks)

    def body(start_ref, *refs):
        for k in range(n):
            at = (start_ref[0] + k) % n
            if inner:
                for i in range(blocks[0].shape[0]):
                    refs[n][i, at] = refs[k][i]
            else:
                refs[n][at] = refs[k][...]

    shape = blocks[0].shape
    shape = (shape[0], n) + shape[1:] if inner else (n,) + shape
    return pl.pallas_call(
        body,
        out_shape=jax.ShapeDtypeStruct(shape, blocks[0].dtype),
        in_specs=[SMEM] + [VMEM] * n,
        out_specs=VMEM,
        compiler_params=PARAMS,
        interpret=INTERPRET,
    )(start.reshape(1), *blocks)


def gather_ring(block, z):
    buf = jnp.zeros((NZ,) + block.shape, block.dtype)
    put = lambda b, v, k: lax.dynamic_update_index_in_dim(b, v, (z + k) % NZ, 0)
    buf = put(buf, block, 0)
    low = high = block
    for k in range(1, NZ // 2):
        low, high = shift_z(low, 1), shift_z(high, -1)
        buf = put(put(buf, low, NZ - k), high, k)
    half = block.shape[0] // 2
    far = jnp.concatenate([shift_z(low[:half], 1), shift_z(high[half:], -1)], 0)
    return put(buf, far, NZ // 2)


def ring_step(parts, up, down, z, k, *tokens):
    n, rows, T = parts.shape
    half = up.shape[0]

    def body(z_ref, up_part, down_part, up_ref, down_ref, *refs):
        up_out, down_out = refs[-2:]
        if half == rows:
            up_out[...] = up_part[0] + up_ref[...]
            down_out[...] = down_part[0] + down_ref[...]
        else:
            up_out[:half] = up_part[0, :half] + up_ref[...]
            up_out[half:] = up_part[0, half:]
            down_out[:half] = down_part[0, :half]
            down_out[half:] = down_part[0, half:] + down_ref[...]

    full = lambda r: pl.BlockSpec((r, T), lambda i, z_ref: (0, 0))
    return pl.pallas_call(
        body,
        grid_spec=pltpu.PrefetchScalarGridSpec(
            num_scalar_prefetch=1,
            grid=(1,),
            in_specs=[
                pl.BlockSpec((1, rows, T), lambda i, z_ref: ((z_ref[0] + k) % n, 0, 0)),
                pl.BlockSpec((1, rows, T), lambda i, z_ref: ((z_ref[0] + n - k) % n, 0, 0)),
                full(half),
                full(half),
            ]
            + [WAIT] * len(tokens),
            out_specs=[full(rows), full(rows)],
        ),
        out_shape=[jax.ShapeDtypeStruct((rows, T), f32)] * 2,
        compiler_params=PARAMS,
        cost_estimate=cost(2 * rows * T, 24 * rows * T),
        interpret=INTERPRET,
    )(z.reshape(1), parts, parts, up, down, *tokens)


def ring_last(parts, up, down, z):
    n, rows, T = parts.shape

    def body(z_ref, part_ref, up_ref, down_ref, out_ref):
        out_ref[...] = part_ref[0] + up_ref[...] + down_ref[...]

    full = pl.BlockSpec((rows, T), lambda i, z_ref: (0, 0))
    return pl.pallas_call(
        body,
        grid_spec=pltpu.PrefetchScalarGridSpec(
            num_scalar_prefetch=1,
            grid=(1,),
            in_specs=[pl.BlockSpec((1, rows, T), lambda i, z_ref: (z_ref[0], 0, 0)), full, full],
            out_specs=full,
        ),
        out_shape=jax.ShapeDtypeStruct((rows, T), f32),
        compiler_params=PARAMS,
        cost_estimate=cost(2 * rows * T, 16 * rows * T),
        interpret=INTERPRET,
    )(z.reshape(1), parts, up, down)


def ring_first(parts, z):
    half = parts.shape[1] // 2
    far = pick(parts, (z + NZ // 2) % NZ)
    return shift_z(far[:half], 1), shift_z(far[half:], -1)


def scatter_ring(parts, up, down, z, *tokens):
    for k in range(NZ // 2 - 1, 0, -1):
        up, down = ring_step(parts, up, down, z, k, *(tokens if k == 1 else ()))
        up, down = shift_z(up, 1), shift_z(down, -1)
    return ring_last(parts, up, down, z)


def by_tok(codes, tok):
    n, (L, T) = len(codes), codes[0].shape
    Q = L // 4

    def body(tok_ref, *refs):
        for i, q in enumerate((0, 2, 1, 3)):
            from_row = pl.multiple_of((tok_ref[0] ^ q) * Q, Q)
            for k in range(n):
                refs[n][pl.ds((i * n + k) * Q, Q), :] = refs[k][pl.ds(from_row, Q), :]

    return pl.pallas_call(
        body,
        out_shape=jax.ShapeDtypeStruct((n * L, T), codes[0].dtype),
        in_specs=[SMEM] + [VMEM] * n,
        out_specs=VMEM,
        compiler_params=PARAMS,
        interpret=INTERPRET,
    )(tok.reshape(1), *codes)


def cost(flops, size):
    return pl.CostEstimate(flops=1, bytes_accessed=1, transcendentals=0)


def dot(a, b, ca, cb):
    return lax.dot_general(a, b, (((ca,), (cb,)), ((), ())), preferred_element_type=f32)


def slabs_of(dec, y, core, token):
    L, D = dec.shape
    C, R = D // (NZ * NX * NY), D // NY

    def body(place_ref, dec_ref, token_ref, *refs):
        outs, scratch = refs[:NY], refs[NY]
        scratch[...] = dec_ref[...].T.astype(f32)
        for k in range(NY):
            at = (place_ref[0] + k) % NY
            for i in range(2):
                rows = [
                    scratch[pl.ds(pl.multiple_of(((i * NX + x) * NY + at) * C, 8), C), :]
                    for x in range(NX)
                ]
                block = jnp.concatenate(rows, 0).astype(bf16)
                if k > 0:
                    block = jnp.where(place_ref[1] == 0, block[:, : L // 2], block[:, L // 2 :])
                outs[k][i * NX * C : (i + 1) * NX * C, :] = block

    widths = [L] + [L // 2] * (NY - 1)
    return pl.pallas_call(
        body,
        grid=(4,),
        out_shape=[jax.ShapeDtypeStruct((R, w), bf16) for w in widths],
        in_specs=[SMEM, pl.BlockSpec((L, D // 4), lambda i: (0, i)), WAIT],
        out_specs=[pl.BlockSpec((R // 4, w), lambda i: (i, 0)) for w in widths],
        scratch_shapes=[pltpu.VMEM((D // 4, L), f32)],
        compiler_params=PARAMS,
        cost_estimate=cost(0, 4 * L * D),
        interpret=INTERPRET,
    )(jnp.stack([y, core]), dec, token)


def join(blocks, token):
    rows, w = blocks[0].shape
    n = len(blocks)

    def body(*refs):
        for k in range(n):
            refs[n + 1][:, k * w : (k + 1) * w] = refs[k][...]

    return pl.pallas_call(
        body,
        grid=(2,),
        out_shape=jax.ShapeDtypeStruct((rows, n * w), blocks[0].dtype),
        in_specs=[pl.BlockSpec((rows // 2, w), lambda i: (i, 0))] * n + [WAIT],
        out_specs=pl.BlockSpec((rows // 2, n * w), lambda i: (i, 0)),
        compiler_params=PARAMS,
        cost_estimate=cost(0, 4 * n * rows * w),
        interpret=INTERPRET,
    )(*blocks, token)


def assemble(own, near, other, core):
    R, L = own.shape
    n, h = len(near), L // 2

    def body(core_ref, own_ref, *refs):
        nears, rest, out = refs[:n], refs[n], refs[n + 1]
        out[:, :L] = own_ref[...]
        for k in range(n):
            mine, his = nears[k][...], rest[:, k * h : (k + 1) * h]
            at = (k + 1) * L
            out[:, at : at + h] = jnp.where(core_ref[0] == 0, mine, his)
            out[:, at + h : at + L] = jnp.where(core_ref[0] == 0, his, mine)

    rows = lambda w: pl.BlockSpec((R // 4, w), lambda i: (i, 0))
    return pl.pallas_call(
        body,
        grid=(4,),
        out_shape=jax.ShapeDtypeStruct((R, (n + 1) * L), own.dtype),
        in_specs=[SMEM, rows(L)] + [rows(h)] * n + [rows(n * h)],
        out_specs=rows((n + 1) * L),
        compiler_params=PARAMS,
        cost_estimate=cost(0, 4 * R * (n + 1) * L),
        interpret=INTERPRET,
    )(core.reshape(1), own, *near, other)


def part_of(decs, codes):
    n, (L, T), R = len(codes), codes[0].shape, decs.shape[0]

    def body(w_ref, *refs):
        refs[n][...] = sum(
            dot(w_ref[:, k * L : (k + 1) * L], refs[k][...], 1, 0) for k in range(n)
        )

    return pl.pallas_call(
        body,
        grid=(4,),
        out_shape=jax.ShapeDtypeStruct((R, T), f32),
        in_specs=[pl.BlockSpec((R // 4, n * L), lambda i: (i, 0))]
        + [pl.BlockSpec((L, T), lambda i: (0, 0))] * n,
        out_specs=pl.BlockSpec((R // 4, T), lambda i: (i, 0)),
        compiler_params=PARAMS,
        cost_estimate=cost(2 * R * n * L * T, 2 * R * n * L + 4 * R * T),
        interpret=INTERPRET,
    )(decs, *codes)


def error_of(total, received, bias, act, xh, scale, *tokens):
    rows, T = total.shape
    C = rows // NX

    def body(xh_ref, total_ref, received_ref, bias_ref, act_ref, *refs):
        value = (total_ref[...] + received_ref[...]) * scale + bias_ref[...]
        value = value - act_ref[...].astype(f32)
        refs[-2][...] = value.astype(bf16)
        refs[-1][...] = jnp.where(xh_ref[0] == 0, value[:C], value[C:]).astype(bf16)

    return pl.pallas_call(
        body,
        out_shape=[jax.ShapeDtypeStruct((r, T), bf16) for r in (rows, C)],
        in_specs=[SMEM] + [VMEM] * 4 + [WAIT] * len(tokens),
        out_specs=[VMEM] * 2,
        compiler_params=PARAMS,
        cost_estimate=cost(4 * rows * T, 16 * rows * T),
        interpret=INTERPRET,
    )(xh.reshape(1), total, received, bias, act, *tokens)


def backs_of(decs, err, n, token):
    (R, W), T = decs.shape, err.shape[1]
    L = W // n

    def body(*refs):
        e = refs[n][...]
        for k in range(n):
            refs[n + 2 + k][...] = dot(refs[k][...], e, 0, 0).astype(bf16)

    return pl.pallas_call(
        body,
        grid=(2,),
        out_shape=[jax.ShapeDtypeStruct((L, T), bf16)] * n,
        in_specs=[pl.BlockSpec((R, L // 2), lambda i, k=k: (0, 2 * k + i)) for k in range(n)]
        + [pl.BlockSpec((R, T), lambda i: (0, 0)), WAIT],
        out_specs=[pl.BlockSpec((L // 2, T), lambda i: (i, 0))] * n,
        compiler_params=PARAMS,
        cost_estimate=cost(2 * R * W * T, 2 * W * (R + T)),
        interpret=INTERPRET,
    )(*([decs] * n), err, token)


def dec_product(err, codes, scale):
    (R, T), W = err.shape, codes.shape[0]

    def body(err_ref, codes_ref, keep_ref, send_ref):
        e = err_ref[...]
        keep_ref[...] = (dot(e, codes_ref[: W // 2, :], 1, 1) * scale).astype(bf16)
        send_ref[...] = (dot(e, codes_ref[W // 2 :, :], 1, 1) * scale).astype(bf16)

    rows = lambda w: pl.BlockSpec((R // 4, w), lambda i: (i, 0))
    return pl.pallas_call(
        body,
        grid=(4,),
        out_shape=[jax.ShapeDtypeStruct((R, W // 2), bf16)] * 2,
        in_specs=[rows(T), pl.BlockSpec((W, T), lambda i: (0, 0))],
        out_specs=[rows(W // 2)] * 2,
        compiler_params=PARAMS,
        cost_estimate=cost(2 * R * W * T, 2 * R * W + 2 * W * T),
        interpret=INTERPRET,
    )(err, codes)


def near_sum(keep, received, token):
    rows, W = keep.shape

    def body(keep_ref, received_ref, token_ref, mine_ref, send_ref):
        total = keep_ref[...].astype(f32) + received_ref[...].astype(f32)
        mine_ref[...] = total[:, : W // 2]
        send_ref[...] = total[:, W // 2 :].astype(bf16)

    block = lambda w: pl.BlockSpec((rows // 4, w), lambda i: (i, 0))
    return pl.pallas_call(
        body,
        grid=(4,),
        out_shape=[jax.ShapeDtypeStruct((rows, W // 2), d) for d in (f32, bf16)],
        in_specs=[block(W), block(W), WAIT],
        out_specs=[block(W // 2), block(W // 2)],
        compiler_params=PARAMS,
        cost_estimate=cost(rows * W, 7 * rows * W),
        interpret=INTERPRET,
    )(keep, received, token)


def far_sum(mine, received, *tokens):
    rows, W = mine.shape
    Q = W // NY

    def body(mine_ref, received_ref, *refs):
        outs = refs[len(tokens) :]
        total = (mine_ref[...] + received_ref[...].astype(f32)).astype(bf16)
        for k in range(NY):
            outs[k][...] = total[:, k * Q : (k + 1) * Q]

    return pl.pallas_call(
        body,
        out_shape=[jax.ShapeDtypeStruct((rows, Q), bf16)] * NY,
        in_specs=[VMEM, VMEM] + [WAIT] * len(tokens),
        out_specs=[VMEM] * NY,
        compiler_params=PARAMS,
        cost_estimate=cost(rows * W, 8 * rows * W),
        interpret=INTERPRET,
    )(mine, received, *tokens)


def grad_of(parts, preact, scale, coef, count, *tokens):
    L, T = preact.shape
    n = len(parts)

    def body(*refs):
        total = refs[0][...].astype(f32)
        for k in range(1, n):
            total = total + refs[k][...].astype(f32)
        grad = (total * scale + coef) / count
        refs[-1][...] = jnp.where(refs[n][...] > 0.0, grad, 0.0).astype(bf16)

    return pl.pallas_call(
        body,
        out_shape=jax.ShapeDtypeStruct((L, T), bf16),
        in_specs=[VMEM] * (n + 1) + [WAIT] * len(tokens),
        out_specs=VMEM,
        compiler_params=PARAMS,
        cost_estimate=cost(8 * L * T, 14 * L * T),
        interpret=INTERPRET,
    )(*parts, preact, *tokens)


def rows_of(act, tok, token):
    D, T = act.shape
    rows = D // 4

    def body(at_ref, act_ref, token_ref, out_ref, sem):
        first = pl.multiple_of(at_ref[0] * rows, rows)
        copy = pltpu.make_async_copy(act_ref.at[pl.ds(first, rows)], out_ref, sem)
        copy.start()
        copy.wait()

    return pl.pallas_call(
        body,
        out_shape=jax.ShapeDtypeStruct((rows, T), act.dtype),
        in_specs=[SMEM, WAIT, WAIT],
        out_specs=WAIT,
        scratch_shapes=[pltpu.SemaphoreType.DMA],
        compiler_params=PARAMS,
        cost_estimate=cost(0, D * T),
        interpret=INTERPRET,
    )(tok.reshape(1), act, token)


def rows_above(act, tok, more, token):
    D, T = act.shape
    rows = D // 4

    def body(at_ref, act_ref, more_ref, token_ref, out_ref, sems):
        first = pl.multiple_of(at_ref[0] * rows, rows)
        copies = [
            pltpu.make_async_copy(
                act_ref.at[pl.ds(first, rows)], out_ref.at[pl.ds(0, rows)], sems.at[0]
            ),
            pltpu.make_async_copy(more_ref, out_ref.at[pl.ds(rows, rows)], sems.at[1]),
        ]
        for copy in copies:
            copy.start()
        for copy in copies:
            copy.wait()

    return pl.pallas_call(
        body,
        out_shape=jax.ShapeDtypeStruct((2 * rows, T), act.dtype),
        in_specs=[SMEM, WAIT, WAIT, WAIT],
        out_specs=WAIT,
        scratch_shapes=[pltpu.SemaphoreType.DMA((2,))],
        compiler_params=PARAMS,
        cost_estimate=cost(0, 2 * D * T),
        interpret=INTERPRET,
    )(tok.reshape(1), act, more, token)


def hold(x, *tokens):
    def body(x_ref, *refs):
        refs[-1][...] = x_ref[...]

    return pl.pallas_call(
        body,
        out_shape=jax.ShapeDtypeStruct(x.shape, x.dtype),
        in_specs=[VMEM] + [WAIT] * len(tokens),
        out_specs=VMEM,
        compiler_params=PARAMS,
        cost_estimate=cost(0, 4 * x.size),
        interpret=INTERPRET,
    )(x, *tokens)


def enc_first(act, tok, act_core, grads):
    (D, T), L = act.shape, grads[0].shape[0]
    rows = D // 16

    def body(tok_ref, act_ref, core_ref, own_grad, core_grad, out_ref):
        out_ref[...] = dot(act_ref[...], own_grad[...], 1, 1) + dot(
            core_ref[...], core_grad[...], 1, 1
        )

    full = pl.BlockSpec((L, T), lambda i, tok_ref: (0, 0))
    return pl.pallas_call(
        body,
        grid_spec=pltpu.PrefetchScalarGridSpec(
            num_scalar_prefetch=1,
            grid=(4,),
            in_specs=[
                pl.BlockSpec((rows, T), lambda i, tok_ref: (tok_ref[0] * 4 + i, 0)),
                pl.BlockSpec((rows, T), lambda i, tok_ref: (i, 0)),
                full,
                full,
            ],
            out_specs=pl.BlockSpec((rows, L), lambda i, tok_ref: (i, 0)),
        ),
        out_shape=jax.ShapeDtypeStruct((4 * rows, L), f32),
        compiler_params=PARAMS,
        cost_estimate=cost(16 * rows * T * L, 16 * rows * L),
        interpret=INTERPRET,
    )(tok.reshape(1), act, act_core, *grads)


def enc_update(first, act_xl, act_core, grads, enc, rate, scale):
    (rows, L), T = first.shape, act_xl.shape[1]

    def body(rate_ref, first_ref, enc_ref, xl_ref, both_ref, xl_grad, both_grad, out_ref):
        total = first_ref[...] + dot(xl_ref[...], xl_grad[...], 1, 1)
        total = total + dot(both_ref[...], both_grad[...], 1, 1)
        step = rate_ref[0] * scale
        out_ref[...] = (enc_ref[...].astype(f32) - step * total).astype(bf16)

    block = lambda w: pl.BlockSpec((rows // 4, w), lambda i: (i, 0))
    full = pl.BlockSpec((L, T), lambda i: (0, 0))
    return pl.pallas_call(
        body,
        grid=(4,),
        in_specs=[
            SMEM,
            block(L),
            block(L),
            block(T),
            pl.BlockSpec((rows // 4, T), lambda i: (4 + i, 0)),
            full,
            full,
        ],
        out_specs=block(L),
        out_shape=jax.ShapeDtypeStruct((rows, L), bf16),
        compiler_params=PARAMS,
        cost_estimate=cost(4 * rows * T * L, 16 * rows * L),
        interpret=INTERPRET,
    )(rate, first, enc, act_xl, act_core, *grads)


def dec_update(grads, dec, tok, y, rate):
    (rows, Q), D = grads[0].shape, dec.shape[1]
    C = D // (NZ * NX * NY)
    n = len(grads)

    def body(at_ref, rate_ref, dec_ref, *refs):
        out, scratch = refs[n:]
        for k in range(n):
            value = refs[k][...].astype(f32)
            to = (at_ref[1] + k) % NY
            for g in range(rows // C):
                row = (g * NY + to) * C
                scratch[pl.ds(pl.multiple_of(row, 8), C), :] = value[g * C : (g + 1) * C]
        step = rate_ref[0]
        for i in range(4):
            at = slice(i * (D // 4), (i + 1) * (D // 4))
            new = dec_ref[:, at].astype(f32) - step * scratch[at, :].T
            out[:, at] = new.astype(bf16)

    full = pl.BlockSpec((rows, Q), lambda i, at_ref: (0, 0))
    return pl.pallas_call(
        body,
        grid_spec=pltpu.PrefetchScalarGridSpec(
            num_scalar_prefetch=1,
            grid=(1,),
            in_specs=[SMEM, pl.BlockSpec((Q, D), lambda i, at_ref: (at_ref[0], 0))]
            + [full] * n,
            out_specs=pl.BlockSpec((Q, D), lambda i, at_ref: (0, 0)),
            scratch_shapes=[pltpu.VMEM((D, Q), f32)],
        ),
        out_shape=jax.ShapeDtypeStruct((Q, D), bf16),
        compiler_params=PARAMS,
        cost_estimate=cost(2 * Q * D, 6 * Q * D),
        interpret=INTERPRET,
    )(jnp.stack([tok, y]), rate, dec, *grads)


def local(activations, enc_weight, enc_bias, dec_weight, dec_bias, learning_rate):
    T = activations.shape[0]
    D, L = enc_weight.shape
    latent_total = L * NZ * NX * NY
    token_total = T * NL * NC
    C = D // (NZ * NX * NY)
    enc_scale = 1.0 / math.sqrt(D)
    dec_scale = 2.0 / math.sqrt(latent_total)
    z, xh, y = lax.axis_index("z"), lax.axis_index("xh"), lax.axis_index("y")
    xl, core = lax.axis_index("xl"), lax.axis_index("core")
    tok = xl * NC + core

    act_t = activations.T
    pair = place([act_t, swap_xh(act_t)], xh)
    quad = place([pair] + [shift_y(pair, -k) for k in range(1, NY)], y, inner=True)
    act = gather_ring(quad.reshape(NX * NY * C, T), z).reshape(D, T)

    R = NZ * NX * C
    slabs = slabs_of(dec_weight, y, core, quad)
    dec_own = slabs[0]
    dec_near = [shift_y(slabs[NY - k], -k) for k in range(1, NY)]

    preact = dot(enc_weight, act, 0, 0) * enc_scale + enc_bias[:, None]
    codes = jnp.maximum(preact, 0.0).astype(bf16)
    codes_all = [codes] + [shift_y(codes, -k) for k in range(1, NY)]
    dec_other = swap_core(join(dec_near, codes))
    decs = assemble(dec_own, dec_near, dec_other, core)

    part = part_of(decs, codes_all)
    act_xl = swap_xl(rows_of(act, tok ^ 2, decs))
    part = part.reshape(NZ, NX * C, T)
    up, down = ring_first(part, z)
    act_far = swap_xl(rows_of(act, tok ^ 3, up))
    codes_rel = by_tok(codes_all, tok)
    bias = dec_bias.reshape(NZ, NX, NY, C)
    bias = pick(pick(bias, z), y, 1).reshape(NX * C, 1)
    total = scatter_ring(part, up, down, z, act_xl, codes_rel, bias)
    rows = rows_above(act, tok ^ 1, act_far, total)
    act_core = swap_core(rows)
    errors, error_own = error_of(
        total, swap_xh(total), bias, pair.reshape(NX * C, T), xh, dec_scale, codes_rel, rows
    )
    error_own = error_own.T
    err = gather_ring(errors, z).reshape(R, T)

    keep, send = dec_product(err, codes_rel, dec_scale / token_total)

    backs = backs_of(decs, err, NY, keep)
    received = [shift_y(backs[k], k) for k in range(1, NY)]

    mine, send = near_sum(keep, swap_core(send), backs[1])
    got = swap_xl(send)
    enc_own = rows_of(enc_weight, tok, mine)
    sums = far_sum(mine, got)
    grad_pre = grad_of(
        [backs[0], *received], preact, dec_scale, sparsity_coef, token_total, sums[0]
    )
    sums = [sums[0]] + [shift_y(sums[k], k) for k in range(1, NY)]
    sums = sums[:1] + sums[:0:-1]

    far = swap_xl(grad_pre)
    first = enc_first(act, tok, act_core, [grad_pre, swap_core(grad_pre)])
    far = hold(far, first, enc_own, *sums[1:])
    rate = learning_rate * math.sqrt(token_total * latent_total)
    new_dec = dec_update(sums, dec_weight, tok, y, rate)
    new_enc = enc_update(
        first, act_xl, act_core, [far, swap_core(far)], enc_own, rate, enc_scale
    )
    return (error_own, new_enc, new_dec)


def solution(mesh):
    fine = Mesh(mesh.devices.reshape(NZ, NX, NY, NL, NC), ("z", "xh", "y", "xl", "core"))
    lat, tok = ("z", "xh", "y"), ("xl", "core")
    in_specs = (P(tok, lat), P(None, lat), P(lat), P(lat, None), P(), P())
    out_specs = (P(tok, lat), P(tok, lat), P(lat + tok, None))
    return jax.shard_map(local, mesh=fine, in_specs=in_specs, out_specs=out_specs, check_vma=False)
```
